256 devices in a mesh: tm: 32 (over x_lo, z, core), state: 8 (over y, x_hi).
Axes of the slice: x: 4 (x_hi: 2, x_lo: 2; x = x_hi * 2 + x_lo), y: 4, z: 8, core: 2. Of those that a mesh axis runs over, the one named last changes fastest.
Arguments:
- transition: float32 [32, 1024, 1024], P('tm', None, 'state'), may hold values from -0.1875 to 0.1875
- control_gram: float32 [32, 1024, 1024], P('tm', None, 'state'), as said below
- value_gram: float32 [32, 1024, 1024], P('tm', None, 'state'), as said below
Outputs:
- joined_transition: float32 [32, 1024, 1024], P('tm', None, 'state')
- joined_control: float32 [32, 1024, 1024], P('tm', None, 'state')
- joined_value: float32 [32, 1024, 1024], P('tm', None, 'state')
The draws below stay inside these ranges and needn't reach their ends.
Inputs may be any that keep to these rules, and one draw needn't show every extreme that they name: `control_gram`: symmetric positive definite; its smallest eigenvalue is 0.25 or more. `value_gram`: symmetric positive definite; its smallest eigenvalue is 0.25 or more.
All inputs are finite; a program needn't handle non-finite values.
Results may differ from the reference program's by a relative error of at most 0.0075.
The reference program's roundings to bfloat16 on the way count: a program that leaves them out, or rounds other values in their place, can miss the bound.
Values may be sent and summed in bfloat16 or wider, within the bound.
No kernel may reach another device: no remote copies, remote signals or barrier semaphores. Data moves between devices by JAX's collectives and lax.ppermute only.
A program may use at most 128 MiB of HBM per device.

```python
import jax
import jax.numpy as jnp
from jax import lax

N = 1024
LEVELS = 1
NT = 32


def gram_from_entries(entries, shift):
    product = jnp.einsum('eik,ejk->eij', entries, entries, precision=lax.Precision.HIGHEST) * (9.0 / N)
    symmetric = 0.5 * (product + jnp.swapaxes(product, 1, 2))
    identity = jnp.eye(N, dtype=jnp.float32)
    return symmetric + shift * identity


def draw_control_gram(key, part):
    key = jax.random.fold_in(key, 11)
    first_key, second_key = jax.random.split(key)
    entries = jax.random.normal(first_key, (NT, N, N), jnp.float32)
    shift = jnp.exp(jax.random.uniform(second_key, (NT, 1, 1), jnp.float32, jnp.log(0.25), 0.0))
    return gram_from_entries(entries, shift)


def draw_value_gram(key, part):
    key = jax.random.fold_in(key, 23)
    first_key, second_key = jax.random.split(key)
    entries = jax.random.normal(first_key, (NT, N, N), jnp.float32)
    shift = jnp.exp(jax.random.uniform(second_key, (NT, 1, 1), jnp.float32, jnp.log(0.25), 0.0))
    return gram_from_entries(entries, shift)


def block_levels(key, extent, cuts, least, top_value):
    gain, own = 1.0, jax.random.fold_in(key, 6)
    for position, parts in cuts:
        heights = jnp.exp(jax.random.uniform(jax.random.fold_in(own, position), (parts,), jnp.float32, least / len(cuts), top_value / len(cuts)))
        gain = gain * jnp.repeat(heights, extent[position] // parts).reshape([-1 if axis == position else 1 for axis in range(len(extent))])
    return gain


def noise(rng, shape, deviation, most, shards=(), kind=jnp.bfloat16):
    factor_of = block_levels(rng, shape, shards, -0.22, 0.18) if shards else 1.0
    array = jax.random.normal(rng, shape, jnp.float32) * deviation * factor_of
    return jnp.minimum(jnp.maximum(array, -most), most).astype(kind)


def setup_inputs(seed: int = 0) -> dict:
    keys = jax.random.split(jax.random.key(seed), 4)
    return {
        "transition": noise(keys[0], (NT, N, N), N ** -0.5, 0.1875, ((0, 32), (2, 8)), jnp.float32),
        "control_gram": draw_control_gram(jax.random.fold_in(keys[3], 71), 0),
        "value_gram": draw_value_gram(jax.random.fold_in(keys[3], 71), 0),
    }


HIGHEST_PRECISION = lax.Precision.HIGHEST

def combine_pair(current, later):
    trans, ctrl, value = current
    later_t, later_c, later_v = later
    matrix_order = trans.shape[0]
    identity = jnp.eye(matrix_order, dtype=jnp.float32)
    trans_b = later_t.astype(jnp.bfloat16)
    value_b = later_v.astype(jnp.bfloat16)
    value_root = lax.linalg.cholesky(value_b.astype(jnp.float32), symmetrize_input=False)
    coupled = jnp.dot(value_root.T, ctrl, precision=HIGHEST_PRECISION)
    inner_gram = identity + jnp.dot(coupled, value_root, precision=HIGHEST_PRECISION)
    inner_root = lax.linalg.cholesky(inner_gram, symmetrize_input=False)
    projected = jnp.dot(value_root.T, trans, precision=HIGHEST_PRECISION)
    value_side = jax.scipy.linalg.solve_triangular(inner_root, projected, lower=True).astype(jnp.bfloat16)
    control_side = jax.scipy.linalg.solve_triangular(inner_root, coupled, lower=True).astype(jnp.bfloat16)
    solved = (trans - jnp.dot(control_side.T.astype(jnp.float32), value_side.astype(jnp.float32), preferred_element_type=jnp.float32)).astype(jnp.bfloat16)
    residual_gram = (ctrl - jnp.dot(control_side.T.astype(jnp.float32), control_side.astype(jnp.float32), preferred_element_type=jnp.float32)).astype(jnp.bfloat16)
    new_value = value + jnp.dot(value_side.T.astype(jnp.float32), value_side.astype(jnp.float32), preferred_element_type=jnp.float32)
    new_trans = jnp.dot(trans_b.astype(jnp.float32), solved.astype(jnp.float32), preferred_element_type=jnp.float32)
    mapped = jnp.dot(residual_gram.astype(jnp.float32), trans_b.T.astype(jnp.float32), preferred_element_type=jnp.float32).astype(jnp.bfloat16)
    new_ctrl = later_c + jnp.dot(trans_b.astype(jnp.float32), mapped.astype(jnp.float32), preferred_element_type=jnp.float32)
    return (new_trans, new_ctrl, new_value)

def reference(transition, control_gram, value_gram):
    element_total = transition.shape[0]
    matrix_order = transition.shape[1]
    identity = jnp.eye(matrix_order, dtype=jnp.float32)
    current = (transition, control_gram, value_gram)
    for section_index in range(LEVELS):
        distance = 2 ** section_index
        pad_eye = jnp.broadcast_to(identity, (distance, matrix_order, matrix_order))
        pad_zero = jnp.zeros((distance, matrix_order, matrix_order), jnp.float32)
        later = (jnp.concatenate([current[0][distance:], pad_eye], 0)[:element_total], jnp.concatenate([current[1][distance:], pad_zero], 0)[:element_total], jnp.concatenate([current[2][distance:], pad_eye], 0)[:element_total])
        joined = lax.map(lambda members_pair: combine_pair(members_pair[0], members_pair[1]), (current, later))
        has_partner = (jnp.arange(element_total) + distance < element_total)[:, None, None]
        current = tuple((jnp.where(has_partner, new_part, old_part) for new_part, old_part in zip(joined, current)))
    return (current[0], current[1], current[2])
```

```python
import functools

import jax
import jax.numpy as jnp
from jax import lax
from jax.experimental import pallas as pl
from jax.experimental.pallas import tpu as pltpu
from jax.sharding import PartitionSpec as P

f32, bf16 = jnp.float32, jnp.bfloat16
B = 128
STEP = 32
VMEM = pl.BlockSpec(memory_space=pltpu.VMEM)
SMEM = pl.BlockSpec(memory_space=pltpu.SMEM)
PARAMS = pltpu.CompilerParams(vmem_limit_bytes=56 << 20)


def halves(x):
    high = x.astype(bf16)
    return high, (x - high.astype(f32)).astype(bf16)


def product(a, b, ca=1, cb=0):
    return lax.dot_general(a, b, (((ca,), (cb,)), ((), ())), preferred_element_type=f32)


def product3(a, b, ca=1, cb=0):
    return product(a[0], b[0], ca, cb) + (product(a[0], b[1], ca, cb) + product(a[1], b[0], ca, cb))


def factor_block(block):
    sub = lax.broadcasted_iota(jnp.int32, (B, B), 0)
    ident = jnp.where(sub == lax.broadcasted_iota(jnp.int32, (B, B), 1), 1.0, 0.0).astype(f32)
    left = jnp.concatenate([block, ident], 1)
    lane = lax.broadcasted_iota(jnp.int32, (STEP, 2 * B), 1)
    row = lax.broadcasted_iota(jnp.int32, (STEP, 2 * B), 0)
    done = []
    for first in range(0, B, STEP):
        work = left[:STEP]
        cols = [
            jnp.broadcast_to(work[:, first + k : first + k + 1], (STEP, B)) for k in range(STEP)
        ]
        rows = []
        for k in range(STEP):
            scale = lax.rsqrt(cols[k][k : k + 1])
            column = cols[k] * scale
            pivot_row = work[k : k + 1] * jnp.concatenate([scale, scale], 1)
            rows.append(pivot_row)
            if k + 1 < STEP:
                for j in range(k + 1, STEP):
                    cols[j] = cols[j] - column * column[j : j + 1]
                work = work - jnp.concatenate([column, column], 1) * pivot_row
        upper = jnp.where(lane >= first + row, jnp.concatenate(rows, 0), 0.0)
        done.append(upper)
        if first + STEP < B:
            high, low = halves(upper)
            right = jnp.concatenate([high, low, high], 0)
            turned = jnp.concatenate([high[:, :B], high[:, :B], low[:, :B]], 0)
            left = left[STEP:] - product(turned, right, 0, 0)[first + STEP :]
    full = jnp.concatenate(done, 0)
    return full[:, :B], full[:, B:]


def eliminate(base, high, low, order, width):
    count = order // B
    current = base(0, 0, width)
    for i in range(count):
        at = i * B
        upper, inverse = factor_block(current[:, :B])
        inverse = halves(inverse)
        high[at : at + B, at : at + B], low[at : at + B, at : at + B] = halves(upper)
        past = at + B
        if i + 1 < count:
            past = at + 2 * B
            near = halves(product3(inverse, halves(current[:, B : 2 * B])))
            high[at : at + B, at + B : past], low[at : at + B, at + B : past] = near
            diagonal = base(i + 1, at + B, past)
            before = (high[:at, at + B : past], low[:at, at + B : past])
            if i > 0:
                diagonal = diagonal - product3(before, before, 0, 0)
            diagonal = diagonal - product3(near, near, 0, 0)
        if past < width:
            far = halves(product3(inverse, halves(current[:, past - at :])))
            high[at : at + B, past:], low[at : at + B, past:] = far
        if i + 1 < count:
            current = diagonal
            if past < width:
                rest = base(i + 1, past, width)
                if i > 0:
                    rest = rest - product3(before, (high[:at, past:], low[:at, past:]), 0, 0)
                current = jnp.concatenate([diagonal, rest - product3(near, far, 0, 0)], 1)


def place(order, blocks, whole):
    for slot, block in enumerate(blocks):
        whole[:, pl.ds(pl.multiple_of(order[slot] * B, B), B)] = block[...]


def value_root_kernel(order, *refs):
    blocks, (high, low, value) = refs[:8], refs[8:]
    place(order, blocks, value)
    n = value.shape[0]
    eliminate(lambda i, a, b: value[i * B : (i + 1) * B, a:b].astype(f32), high, low, n, n)


def inner_kernel(order, root_high, root_low, *refs):
    blocks, (trans, u_out, h_out, side_high, side_low, base, high, low) = refs[:8], refs[8:]
    n = root_high.shape[0]
    for slot, block in enumerate(blocks):
        at = pl.ds(pl.multiple_of(order[slot] * B, B), B)
        side_high[:, at], side_low[:, at] = halves(block[...])
    side_high[:, n:], side_low[:, n:] = halves(trans[...])
    for i in range(n // B):
        at, end = i * B, (i + 1) * B
        coupled = product3(
            (root_high[at:end, at:], root_low[at:end, at:]), (side_high[at:, :], side_low[at:, :])
        )
        base[at:end, n:] = coupled
        high[at:end, n:], low[at:end, n:] = halves(coupled)
    for j in range(n // B):
        at, end = j * B, (j + 1) * B
        gram = product3(
            (high[:end, n + at : 2 * n], low[:end, n + at : 2 * n]),
            (root_high[at:end, at:], root_low[at:end, at:]),
            1,
            1,
        )
        sub = lax.broadcasted_iota(jnp.int32, (end, B), 0)
        lane = lax.broadcasted_iota(jnp.int32, (end, B), 1)
        base[:end, at:end] = gram + jnp.where(sub == lane + at, 1.0, 0.0)
    eliminate(lambda i, a, b: base[i * B : (i + 1) * B, a:b], high, low, n, base.shape[1])
    u_out[...] = high[:, n : 2 * n]
    h_out[...] = high[:, 2 * n :]


def join_kernel(order, keep, u, h, trans, ctrl, later_c, *refs):
    ctrl_blocks, later_blocks = refs[:8], refs[8:16]
    trans_out, ctrl_out, whole_c, whole_t, gram = refs[16:]
    n = u.shape[0]
    place(order, ctrl_blocks, whole_c)
    place(order, later_blocks, whole_t)
    kept = keep[0] > 0
    solved = (trans[...] - product(u[...], h[...], 0, 0)).astype(bf16)
    for at in range(0, n, B):
        gram[at : at + B, :] = (
            whole_c[at : at + B, :] - product(u[:, at : at + B], u[...], 0, 0)
        ).astype(bf16)
    rows = whole_t[pl.ds(pl.multiple_of(order[0] * B, B), B), :]
    mapped = product(gram[...], rows, 1, 1).astype(bf16)
    trans_out[...] = jnp.where(kept, trans[...], product(whole_t[...], solved))
    ctrl_out[...] = jnp.where(kept, ctrl[...], later_c[...].astype(f32) + product(whole_t[...], mapped))


def value_kernel(order, keep, value, *refs):
    blocks, value_out = refs[:8], refs[8]
    own = blocks[0][...]
    kept = keep[0] > 0
    for slot, block in enumerate(blocks):
        at = pl.ds(pl.multiple_of(order[slot] * B, B), B)
        value_out[at, :] = jnp.where(kept, 0.0, product(block[...], own, 0, 0)) + value[at, :]


def call(kernel, outs, scratch, flops, smem, *args):
    return pl.pallas_call(
        kernel,
        out_shape=[jax.ShapeDtypeStruct(shape, kind) for shape, kind in outs],
        in_specs=[SMEM] * smem + [VMEM] * (len(args) - smem),
        out_specs=[VMEM] * len(outs),
        scratch_shapes=[pltpu.VMEM(shape, kind) for shape, kind in scratch],
        compiler_params=PARAMS,
        cost_estimate=pl.CostEstimate(flops=flops, bytes_accessed=1 << 20, transcendentals=0),
    )(*args)


def gather(block):
    received, source = [block], [lax.axis_index("state")]
    y, x = source[0] // 2, source[0] % 2
    for hop, turn in ((1, 0), (3, 0), (0, 1), (2, 0), (1, 1), (3, 1), (2, 1)):
        route = [(s, (s // 2 + hop) % 4 * 2 + (s + turn) % 2) for s in range(8)]
        received.append(lax.ppermute(block, "state", route))
        source.append((y - hop + 4) % 4 * 2 + (x + turn) % 2)
    return received, jnp.stack(source).astype(jnp.int32)


def per_device(transition, control_gram, value_gram):
    trans, ctrl, value = transition[0], control_gram[0], value_gram[0]
    n = trans.shape[0]
    count = lax.axis_size("tm")
    back = [((t + 1) % count, t) for t in range(count)]
    keep = (lax.axis_index("tm") == count - 1).astype(jnp.int32)[None]
    later_v = lax.ppermute(value.astype(bf16), "tm", back)
    value_blocks, order = gather(later_v)
    value_blocks, ctrl = lax.optimization_barrier((value_blocks, ctrl))
    ctrl_blocks, _ = gather(ctrl)
    root = call(
        value_root_kernel, [((n, n), bf16)] * 2, [((n, n), bf16)], 3 * 10**10, 1, order, *value_blocks
    )
    later_t = lax.ppermute(trans.astype(bf16), "tm", back)
    later_c = lax.ppermute(ctrl.astype(bf16), "tm", back)
    later_blocks, _ = gather(later_t)
    wide = n + B
    u, h = call(
        inner_kernel,
        [((n, n), bf16), ((n, B), bf16)],
        [((n, wide), bf16)] * 2 + [((n, n + wide), f32)] + [((n, n + wide), bf16)] * 2,
        6 * 10**10, 1, order, *root, *ctrl_blocks, trans,
    )
    h_blocks, _ = gather(h)
    new_trans, new_ctrl = call(
        join_kernel,
        [((n, B), f32)] * 2,
        [((n, n), f32), ((n, n), bf16), ((n, n), bf16)],
        10**10, 2, order, keep, u, h, trans, ctrl, later_c, *ctrl_blocks, *later_blocks,
    )
    (new_value,) = call(value_kernel, [((n, B), f32)], [], 10**9, 2, order, keep, value, *h_blocks)
    return new_trans[None], new_ctrl[None], new_value[None]


def solution(mesh):
    placed = (P("tm", None, "state"), P("tm", None, "state"), P("tm", None, "state"))
    return jax.shard_map(
        per_device, mesh=mesh, in_specs=placed, out_specs=placed, check_vma=False
    )
```

```python
import functools

import jax
import jax.numpy as jnp
from jax import lax
from jax.experimental import pallas as pl
from jax.experimental.pallas import tpu as pltpu
from jax.sharding import PartitionSpec as P

f32, bf16 = jnp.float32, jnp.bfloat16
B = 128
STEP = 32
CHUNK = 256
VMEM = pl.BlockSpec(memory_space=pltpu.VMEM)
SMEM = pl.BlockSpec(memory_space=pltpu.SMEM)


def halves(x):
    high = x.astype(bf16)
    return high, (x - high.astype(f32)).astype(bf16)


def product(a, b, ca=1, cb=0):
    return lax.dot_general(a, b, (((ca,), (cb,)), ((), ())), preferred_element_type=f32)


def product3(a, b, ca=1, cb=0):
    return product(a[0], b[0], ca, cb) + (product(a[0], b[1], ca, cb) + product(a[1], b[0], ca, cb))


def factor_block(block, work=()):
    sub = lax.broadcasted_iota(jnp.int32, (B, B), 0)
    ident = jnp.where(sub == lax.broadcasted_iota(jnp.int32, (B, B), 1), 1.0, 0.0).astype(f32)
    left = jnp.concatenate([block, ident], 1)
    lane = lax.broadcasted_iota(jnp.int32, (STEP, 2 * B), 1)
    row = lax.broadcasted_iota(jnp.int32, (STEP, 2 * B), 0)
    done, given = [], 0
    for first in range(0, B, STEP):
        piece = left[:STEP]
        cols = [
            jnp.broadcast_to(piece[:, first + k : first + k + 1], (STEP, B)) for k in range(STEP)
        ]
        rows = []
        for k in range(STEP):
            scale = lax.rsqrt(cols[k][k : k + 1])
            column = cols[k] * scale
            pivot_row = piece[k : k + 1] * jnp.concatenate([scale, scale], 1)
            rows.append(pivot_row)
            if k + 1 < STEP:
                for j in range(k + 1, STEP):
                    cols[j] = cols[j] - column * column[j : j + 1]
                piece = piece - jnp.concatenate([column, column], 1) * pivot_row
            while given < len(work) * (first + k + 1) // B:
                work[given]()
                given += 1
        upper = jnp.where(lane >= first + row, jnp.concatenate(rows, 0), 0.0)
        done.append(upper)
        if first + STEP < B:
            high, low = halves(upper)
            right = jnp.concatenate([high, low, high], 0)
            turned = jnp.concatenate([high[:, :B], high[:, :B], low[:, :B]], 0)
            left = left[STEP:] - product(turned, right, 0, 0)[first + STEP :]
    full = jnp.concatenate(done, 0)
    return full[:, :B], full[:, B:]


def chunks(first, last):
    return [(a, min(a + CHUNK, last)) for a in range(first, last, CHUNK)]


def eliminate(rows, high, low, turned, order, base, finished=None, inverses=None):
    count, width = order // B, rows.shape[1]
    for piece in base(0):
        piece()
    diagonal, work = rows[:B, :B], base(1)
    for i in range(count):
        at, end = i * B, (i + 1) * B
        upper, inverse = factor_block(diagonal, work)
        work = []
        inverse = halves(inverse)
        if inverses is not None:
            inverses[0][i], inverses[1][i] = inverse
        high[at:end, at:end], low[at:end, at:end] = halves(upper)
        past, near_turned = end, None
        if i + 1 < count:
            past = end + B
            near = halves(product3(inverse, halves(rows[at:end, end:past])))
            high[at:end, end:past], low[at:end, end:past] = near
            near_turned = (near[0].T, near[1].T)
            diagonal = rows[end:past, end:past] - product3(near_turned, near)

        def far(a, b, at=at, end=end, inverse=inverse, near_turned=near_turned):
            part = halves(product3(inverse, halves(rows[at:end, a:b])))
            high[at:end, a:b], low[at:end, a:b] = part
            if near_turned is not None:
                rows[end : end + B, a:b] = rows[end : end + B, a:b] - product3(near_turned, part)

        work += [functools.partial(far, a, b) for a, b in chunks(past, width)]
        if i + 2 < count:
            work += base(i + 2)
            c = slice(end + B, end + 2 * B)

            def turn(end=end, c=c):
                turned[0][:, :end], turned[1][:, :end] = high[:end, c].T, low[:end, c].T

            def before(a, b, end=end, c=c):
                left = (turned[0][:, :end], turned[1][:, :end])
                rows[c, a:b] = rows[c, a:b] - product3(left, (high[:end, a:b], low[:end, a:b]))

            work.append(turn)
            work += [functools.partial(before, a, b) for a, b in chunks(end + B, width)]
        if finished is not None:
            work += finished(i)
    for piece in work:
        piece()


def block_at(k):
    return pl.ds(pl.multiple_of(k * B, B), B)


def place(order, slabs, store):
    count = order.shape[0]
    share = count // 2 + 1
    for slot in range(count):
        k = order[slot]
        slab = slabs[slot // 2]
        for t in range(share):
            first = (slot % 2 * share + t) * B
            block = slab[first : first + B, :]
            j = lax.rem(k + t, count)
            store(j, k, block)
            if 0 < t < count // 2:
                store(k, j, block.T)


def value_root_kernel(order, *refs):
    slabs, (high, low, value, rows, turned_high, turned_low) = refs[:-6], refs[-6:]
    n = value.shape[0]

    def store(j, k, block):
        value[block_at(j), block_at(k)] = block

    place(order, slabs, store)

    def base(i):
        def widen():
            rows[i * B : (i + 1) * B, i * B :] = value[i * B : (i + 1) * B, i * B :].astype(f32)

        return [widen]

    eliminate(rows, high, low, (turned_high, turned_low), n, base)


def inner_kernel(order, root_high, root_low, trans, *refs):
    slabs, refs = refs[:4], refs[4:]
    gram_out, solved_out, back_out = refs[:3]
    gram, side_high, side_low, rows, high, low, turned_high, turned_low = refs[3:11]
    left_high, left_low, inverse_high, inverse_low, back_high, back_low = refs[11:]
    n = root_high.shape[0]
    count = n // B

    def store(j, k, block):
        gram[block_at(j), block_at(k)] = block
        side_high[block_at(j), block_at(k)], side_low[block_at(j), block_at(k)] = halves(block)

    place(order, slabs, store)
    side_high[:, n:], side_low[:, n:] = halves(trans[...])
    sub = lax.broadcasted_iota(jnp.int32, (B, B), 0)
    ident = jnp.where(sub == lax.broadcasted_iota(jnp.int32, (B, B), 1), 1.0, 0.0).astype(f32)

    def base(i):
        at, end = i * B, (i + 1) * B

        def couple(a, b):
            part = product3(
                (root_high[at:end, at:], root_low[at:end, at:]),
                (side_high[at:, a:b], side_low[at:, a:b]),
            )
            rows[at:end, n + a : n + b] = part
            if a < n:
                left_high[:, a:b], left_low[:, a:b] = halves(part)

        def inner(j):
            c = slice(j * B, (j + 1) * B)
            part = product3(
                (left_high[:, j * B :], left_low[:, j * B :]),
                (root_high[c, j * B :], root_low[c, j * B :]),
                1,
                1,
            )
            rows[at:end, c] = part + ident if j == i else part

        work = [functools.partial(couple, a, b) for a, b in chunks(0, n + B)]
        return work + [functools.partial(inner, j) for j in range(i, count)]

    def subtract(first, last, r, out):
        c = slice(r, r + B)
        out[c, :] = (
            gram[c, :] - product(high[first:last, n + r : n + r + B], high[first:last, n : 2 * n], 0, 0)
        ).astype(out.dtype)

    def finished(i):
        first, last = (i - 1) * B, (i + 1) * B
        if i == count - 2:
            first = i * B
        elif i % 2 == 0 or i == count - 1:
            return []
        return [functools.partial(subtract, first, last, r, gram) for r in range(0, n, B)]

    eliminate(
        rows, high, low, (turned_high, turned_low), n, base, finished, (inverse_high, inverse_low)
    )

    def solve(a, b):
        solved_out[:, a:b] = (
            trans[a:b, :].T - product(high[:, 2 * n :], high[:, n + a : n + b], 0, 0)
        ).astype(bf16)

    for i in reversed(range(count)):
        at, end = i * B, (i + 1) * B
        part = high[at:end, 2 * n :].T.astype(f32)
        if end < n:
            done = (back_high[:, end:], back_low[:, end:])
            part = part - product3(done, (high[at:end, end:n], low[at:end, end:n]), 1, 1)
        back_high[:, at:end], back_low[:, at:end] = halves(
            product3(halves(part), (inverse_high[i], inverse_low[i]))
        )
        subtract(n - B, n, at, gram_out)
        if i % 2 == 0:
            solve(at, at + 2 * B)
    for j in range(count):
        end = (j + 1) * B
        c = slice(j * B, end)
        back_out[:, c] = product3(
            (back_high[:, :end], back_low[:, :end]), (root_high[:end, c], root_low[:end, c])
        ).astype(bf16)


def join_kernel(state, keep, gram, solved, back, trans, ctrl, value, later_c, both_t, *outs):
    trans_out, ctrl_out, value_out = outs
    kept = keep[0] > 0
    mapped = product(both_t[1, block_at(state[0]), :], gram[...]).astype(bf16)
    joined = product(both_t[1], jnp.concatenate([solved[...], mapped], 0), 1, 1)
    trans_out[...] = jnp.where(kept, trans[...], joined[:, :B])
    ctrl_out[...] = jnp.where(kept, ctrl[...], later_c[...].astype(f32) + joined[:, B:])
    added = product(back[...], both_t[0]).T
    value_out[...] = jnp.where(kept, 0.0, added) + value[...]


def call(kernel, outs, scratch, megabytes, flops, smem, *args):
    return pl.pallas_call(
        kernel,
        out_shape=[jax.ShapeDtypeStruct(shape, kind) for shape, kind in outs],
        in_specs=[SMEM] * smem + [VMEM] * (len(args) - smem),
        out_specs=[VMEM] * len(outs),
        scratch_shapes=[pltpu.VMEM(shape, kind) for shape, kind in scratch],
        compiler_params=pltpu.CompilerParams(vmem_limit_bytes=megabytes << 20),
        cost_estimate=pl.CostEstimate(flops=flops, bytes_accessed=1 << 20, transcendentals=0),
    )(*args)


def turn(s):
    return s // 2 * 2 + (s + 1) % 2


def along(pair):
    return [
        lax.ppermute(pair, "state", [(s, (s // 2 + hop) % 4 * 2 + s % 2) for s in range(8)])
        for hop in (1, 3, 2)
    ]


def sources():
    state = lax.axis_index("state")
    y, x = state // 2, state % 2
    found = []
    for hop in (0, 1, 3, 2):
        found += [(y - hop + 4) % 4 * 2 + x, (y - hop + 4) % 4 * 2 + 1 - x]
    return jnp.stack(found).astype(jnp.int32)


def per_device(transition, control_gram, value_gram):
    trans, ctrl, value = transition[0], control_gram[0], value_gram[0]
    n = trans.shape[0]
    count = lax.axis_size("tm")
    back = [((t + 1) % count, t) for t in range(count)]
    back_turned = [
        ((t + 1) % count * 8 + turn(s), t * 8 + s) for t in range(count) for s in range(8)
    ]
    keep = (lax.axis_index("tm") == count - 1).astype(jnp.int32)[None]
    state = lax.axis_index("state").astype(jnp.int32)
    order = sources()

    def slab(whole):
        around = jnp.concatenate([whole, whole[: n // 2]], 0)
        return lax.dynamic_slice(around, (state * B, 0), (n // 2 + B, B))

    value_slab, ctrl_slab = slab(value.astype(bf16)), slab(ctrl)
    later_v = [
        lax.ppermute(value_slab, "tm", back),
        lax.ppermute(value_slab, ("tm", "state"), back_turned),
    ]
    ctrl_turned = lax.ppermute(ctrl_slab, "state", [(s, turn(s)) for s in range(8)])
    ends = jnp.concatenate([trans.astype(bf16), ctrl.astype(bf16)], 0)
    later = lax.ppermute(ends, "tm", back)
    both_t = jnp.stack([ends[:n], later[:n]])
    later_v, both_t = lax.optimization_barrier((later_v, both_t))
    both_t = lax.all_gather(both_t, "state", axis=2, tiled=True)
    value_pair = jnp.concatenate(later_v, 0)
    value_pairs = [value_pair] + along(value_pair)
    ctrl_pair = jnp.concatenate([ctrl_slab, ctrl_turned], 0)
    ctrl_pairs = [ctrl_pair] + along(ctrl_pair)
    root = call(
        value_root_kernel,
        [((n, n), bf16)] * 2,
        [((n, n), bf16), ((n, n), f32)] + [((B, n), bf16)] * 2,
        24, 3 * 10**10, 1, order, *value_pairs,
    )
    wide = n + B
    gram, solved, back_side = call(
        inner_kernel,
        [((n, n), bf16), ((B, n), bf16), ((B, n), bf16)],
        [((n, n), f32)] + [((n, wide), bf16)] * 2
        + [((n, n + wide), f32)] + [((n, n + wide), bf16)] * 2 + [((B, n), bf16)] * 2
        + [((B, n), bf16)] * 2 + [((n // B, B, B), bf16)] * 2 + [((B, n), bf16)] * 2,
        50, 4 * 10**10, 1, order, *root, trans, *ctrl_pairs,
    )
    new_trans, new_ctrl, new_value = call(
        join_kernel, [((n, B), f32)] * 3, [], 20, 10**10, 2,
        state[None], keep, gram, solved, back_side, trans, ctrl, value, later[n:], both_t,
    )
    return new_trans[None], new_ctrl[None], new_value[None]


def solution(mesh):
    placed = (P("tm", None, "state"), P("tm", None, "state"), P("tm", None, "state"))
    return jax.shard_map(
        per_device, mesh=mesh, in_specs=placed, out_specs=placed, check_vma=False
    )
```

```python
import functools

import jax
import jax.numpy as jnp
from jax import lax
from jax.experimental import pallas as pl
from jax.experimental.pallas import tpu as pltpu
from jax.sharding import PartitionSpec as P

f32, bf16 = jnp.float32, jnp.bfloat16
B = 128
STEP = 32
CHUNK = 256
VMEM = pl.BlockSpec(memory_space=pltpu.VMEM)
SMEM = pl.BlockSpec(memory_space=pltpu.SMEM)


def halves(x):
    high = x.astype(bf16)
    return high, (x - high.astype(f32)).astype(bf16)


def product(a, b, ca=1, cb=0):
    return lax.dot_general(a, b, (((ca,), (cb,)), ((), ())), preferred_element_type=f32)


def product3(a, b, ca=1, cb=0):
    return product(a[0], b[0], ca, cb) + (product(a[0], b[1], ca, cb) + product(a[1], b[0], ca, cb))


def factor_block(block, work=()):
    sub = lax.broadcasted_iota(jnp.int32, (B, B), 0)
    ident = jnp.where(sub == lax.broadcasted_iota(jnp.int32, (B, B), 1), 1.0, 0.0).astype(f32)
    left = jnp.concatenate([block, ident], 1)
    lane = lax.broadcasted_iota(jnp.int32, (STEP, 2 * B), 1)
    row = lax.broadcasted_iota(jnp.int32, (STEP, 2 * B), 0)
    done, given = [], 0
    for first in range(0, B, STEP):
        piece = left[:STEP]
        cols = [
            jnp.broadcast_to(piece[:, first + k : first + k + 1], (STEP, B)) for k in range(STEP)
        ]
        rows = []
        for k in range(STEP):
            scale = lax.rsqrt(cols[k][k : k + 1])
            column = cols[k] * scale
            pivot_row = piece[k : k + 1] * jnp.concatenate([scale, scale], 1)
            rows.append(pivot_row)
            if k + 1 < STEP:
                for j in range(k + 1, STEP):
                    cols[j] = cols[j] - column * column[j : j + 1]
                piece = piece - jnp.concatenate([column, column], 1) * pivot_row
            while given < len(work) * (first + k + 1) // B:
                work[given]()
                given += 1
        upper = jnp.where(lane >= first + row, jnp.concatenate(rows, 0), 0.0)
        done.append(upper)
        if first + STEP < B:
            high, low = halves(upper)
            right = jnp.concatenate([high, low, high], 0)
            turned = jnp.concatenate([high[:, :B], high[:, :B], low[:, :B]], 0)
            left = left[STEP:] - product(turned, right, 0, 0)[first + STEP :]
    full = jnp.concatenate(done, 0)
    return full[:, :B], full[:, B:]


def chunks(first, last):
    return [(a, min(a + CHUNK, last)) for a in range(first, last, CHUNK)]


def eliminate(rows, high, low, turned, order, base, lead, finished=None, inverses=None):
    count, width = order // B, rows.shape[1]
    first_row = base(0)
    for piece in first_row[:lead]:
        piece()
    diagonal, work = rows[:B, :B], first_row[lead:] + base(1)
    for i in range(count):
        at, end = i * B, (i + 1) * B
        upper, inverse = factor_block(diagonal, work)
        work = []
        inverse = halves(inverse)
        if inverses is not None:
            inverses[0][i], inverses[1][i] = inverse
        high[at:end, at:end], low[at:end, at:end] = halves(upper)
        past, near_turned = end, None
        if i + 1 < count:
            past = end + B
            near = halves(product3(inverse, halves(rows[at:end, end:past])))
            high[at:end, end:past], low[at:end, end:past] = near
            near_turned = (near[0].T, near[1].T)
            diagonal = rows[end:past, end:past] - product3(near_turned, near)

        def far(a, b, at=at, end=end, inverse=inverse, near_turned=near_turned):
            part = halves(product3(inverse, halves(rows[at:end, a:b])))
            high[at:end, a:b], low[at:end, a:b] = part
            if near_turned is not None:
                rows[end : end + B, a:b] = rows[end : end + B, a:b] - product3(near_turned, part)

        work += [functools.partial(far, a, b) for a, b in chunks(past, width)]
        if i + 2 < count:
            work += base(i + 2)
            c = slice(end + B, end + 2 * B)

            def turn(end=end, c=c):
                turned[0][:, :end], turned[1][:, :end] = high[:end, c].T, low[:end, c].T

            def before(a, b, end=end, c=c):
                left = (turned[0][:, :end], turned[1][:, :end])
                rows[c, a:b] = rows[c, a:b] - product3(left, (high[:end, a:b], low[:end, a:b]))

            work.append(turn)
            work += [functools.partial(before, a, b) for a, b in chunks(end + B, width)]
        if finished is not None:
            work += finished(i)
    return work


def block_at(k):
    return pl.ds(pl.multiple_of(k * B, B), B)


def place(order, slabs, store):
    count = order.shape[0]
    share = count // 2 + 1
    for slot in range(count):
        k = order[slot]
        slab = slabs[slot // 2]
        for t in range(share):
            first = (slot % 2 * share + t) * B
            block = slab[first : first + B, :]
            j = lax.rem(k + t, count)
            store(j, k, block)
            if 0 < t < count // 2:
                store(k, j, block.T)


def value_root_kernel(order, *refs):
    slabs, (high, low, value, rows, turned_high, turned_low) = refs[:-6], refs[-6:]
    n = value.shape[0]

    def store(j, k, block):
        value[block_at(j), block_at(k)] = block

    place(order, slabs, store)

    def base(i):
        def widen():
            rows[i * B : (i + 1) * B, i * B :] = value[i * B : (i + 1) * B, i * B :].astype(f32)

        return [widen]

    eliminate(rows, high, low, (turned_high, turned_low), n, base, 1)


def inner_kernel(order, root_high, root_low, trans, *refs):
    slabs, refs = refs[:4], refs[4:]
    gram_out, solved_out, back_out = refs[:3]
    gram, side_high, side_low, rows, high, low, turned_high, turned_low = refs[3:11]
    left_high, left_low, inverse_high, inverse_low, back_high, back_low, back = refs[11:]
    n = root_high.shape[0]
    count = n // B

    def store(j, k, block):
        gram[block_at(j), block_at(k)] = block
        side_high[block_at(j), block_at(k)], side_low[block_at(j), block_at(k)] = halves(block)

    place(order, slabs, store)
    side_high[:, n:], side_low[:, n:] = halves(trans[...])
    sub = lax.broadcasted_iota(jnp.int32, (B, B), 0)
    ident = jnp.where(sub == lax.broadcasted_iota(jnp.int32, (B, B), 1), 1.0, 0.0).astype(f32)

    def base(i):
        at, end = i * B, (i + 1) * B

        def couple(a, b):
            part = product3(
                (root_high[at:end, at:], root_low[at:end, at:]),
                (side_high[at:, a:b], side_low[at:, a:b]),
            )
            rows[at:end, n + a : n + b] = part
            if a < n:
                left_high[:, a:b], left_low[:, a:b] = halves(part)

        def inner(j):
            c = slice(j * B, (j + 1) * B)
            part = product3(
                (left_high[:, j * B :], left_low[:, j * B :]),
                (root_high[c, j * B :], root_low[c, j * B :]),
                1,
                1,
            )
            rows[at:end, c] = part + ident if j == i else part

        work = [functools.partial(couple, a, b) for a, b in chunks(0, n)]
        work += [functools.partial(inner, j) for j in range(i, count)]
        return work + [functools.partial(couple, n, n + B)]

    def subtract(first, last, r, out):
        c = slice(r, r + B)
        out[c, :] = (
            gram[c, :] - product(high[first:last, n + r : n + r + B], high[first:last, n : 2 * n], 0, 0)
        ).astype(out.dtype)

    def finished(i):
        first, last = (i - 1) * B, (i + 1) * B
        if i == count - 2:
            first = i * B
        elif i % 2 == 0 or i == count - 1:
            return []
        return [functools.partial(subtract, first, last, r, gram) for r in range(0, n, B)]

    work = eliminate(
        rows, high, low, (turned_high, turned_low), n, base, len(chunks(0, n)) + 1, finished,
        (inverse_high, inverse_low),
    )

    def solve(a, b):
        solved_out[:, a:b] = (
            trans[a:b, :].T - product(high[:, 2 * n :], high[:, n + a : n + b], 0, 0)
        ).astype(bf16)

    def behind(i, j):
        part = (back_high[:, j * B :], back_low[:, j * B :])
        c = slice(i * B, (i + 1) * B)
        return product3(part, (high[c, j * B : n], low[c, j * B : n]), 1, 1)

    work.pop()()
    work += [functools.partial(subtract, n - B, n, r, gram_out) for r in range(0, n, B)]
    work += [functools.partial(solve, a, b) for a, b in chunks(0, n)]
    share = -(-len(work) // count)
    part = high[n - B : n, 2 * n :].T.astype(f32)
    for i in reversed(range(count)):
        at, end = i * B, (i + 1) * B
        later_part = None
        if i > 0:
            later_part = high[at - B : at, 2 * n :].T.astype(f32)
            if end < n:
                later_part = later_part - behind(i - 1, i + 1)
        found = halves(product3(halves(part), (inverse_high[i], inverse_low[i])))
        back_high[:, at:end], back_low[:, at:end] = found
        if i > 0:
            c = slice(at - B, at)
            part = later_part - product3(found, (high[c, at:end], low[c, at:end]), 1, 1)
        added = product3(found, (root_high[at:end, at:], root_low[at:end, at:]))
        if end < n:
            back[:, at:end] = added[:, :B]
            back[:, end:] = back[:, end:] + added[:, B:]
        else:
            back[:, at:] = added
        for piece in work[:share]:
            piece()
        work = work[share:]
    back_out[...] = back[...].astype(bf16)


def join_kernel(order, keep, gram, solved, back, trans, ctrl, value, later_c, whole_t, *refs):
    pairs, (trans_out, ctrl_out, value_out, later_t) = refs[:-4], refs[-4:]
    n = trans.shape[0]
    kept = keep[0] > 0
    for slot in range(order.shape[0]):
        block = pairs[slot // 2][slot % 2 * n : (slot % 2 + 1) * n, :]
        later_t[:, block_at(order[slot])] = block
    mapped = product(later_t[block_at(order[0]), :], gram[...]).astype(bf16)
    joined = product(later_t[...], jnp.concatenate([solved[...], mapped], 0), 1, 1)
    trans_out[...] = jnp.where(kept, trans[...], joined[:, :B])
    ctrl_out[...] = jnp.where(kept, ctrl[...], later_c[...].astype(f32) + joined[:, B:])
    added = product(back[...], whole_t[...]).T
    value_out[...] = jnp.where(kept, 0.0, added) + value[...]


def slab_kernel(order, whole, out):
    count = order.shape[0]
    for t in range(count // 2 + 1):
        out[t * B : (t + 1) * B, :] = whole[block_at(lax.rem(order[0] + t, count)), :].astype(out.dtype)


def call(kernel, outs, scratch, megabytes, flops, smem, *args):
    return pl.pallas_call(
        kernel,
        out_shape=[jax.ShapeDtypeStruct(shape, kind) for shape, kind in outs],
        in_specs=[SMEM] * smem + [VMEM] * (len(args) - smem),
        out_specs=[VMEM] * len(outs),
        scratch_shapes=[pltpu.VMEM(shape, kind) for shape, kind in scratch],
        compiler_params=pltpu.CompilerParams(vmem_limit_bytes=megabytes << 20),
        cost_estimate=pl.CostEstimate(flops=flops, bytes_accessed=1 << 20, transcendentals=0),
    )(*args)


def turn(s):
    return s // 2 * 2 + (s + 1) % 2


def along(pair):
    return [
        lax.ppermute(pair, "state", [(s, (s // 2 + hop) % 4 * 2 + s % 2) for s in range(8)])
        for hop in (1, 3, 2)
    ]


def sources():
    state = lax.axis_index("state")
    y, x = state // 2, state % 2
    found = []
    for hop in (0, 1, 3, 2):
        found += [(y - hop + 4) % 4 * 2 + x, (y - hop + 4) % 4 * 2 + 1 - x]
    return jnp.stack(found).astype(jnp.int32)


def per_device(transition, control_gram, value_gram):
    trans, ctrl, value = transition[0], control_gram[0], value_gram[0]
    n = trans.shape[0]
    count = lax.axis_size("tm")
    back = [((t + 1) % count, t) for t in range(count)]
    back_turned = [
        ((t + 1) % count * 8 + turn(s), t * 8 + s) for t in range(count) for s in range(8)
    ]
    keep = (lax.axis_index("tm") == count - 1).astype(jnp.int32)[None]
    order = sources()
    turned = [(s, turn(s)) for s in range(8)]

    def slab(whole, kind):
        (share,) = call(slab_kernel, [((n // 2 + B, B), kind)], [], 16, 10**8, 1, order, whole)
        return share

    value_slab = slab(value, bf16)
    later_v = [
        lax.ppermute(value_slab, "tm", back),
        lax.ppermute(value_slab, ("tm", "state"), back_turned),
    ]
    ctrl_slab = slab(ctrl, f32)
    ctrl_turned = lax.ppermute(ctrl_slab, "state", turned)
    later_v, late_trans, late_ctrl = lax.optimization_barrier((later_v, trans, ctrl))
    trans_b = late_trans.astype(bf16)
    whole_t = lax.all_gather(trans_b, "state", axis=1, tiled=True)
    value_pair = jnp.concatenate(later_v, 0)
    value_pairs = [value_pair] + along(value_pair)
    later = lax.ppermute(jnp.concatenate([trans_b, late_ctrl.astype(bf16)], 0), "tm", back)
    later_turned = lax.ppermute(trans_b, ("tm", "state"), back_turned)
    trans_pair = jnp.concatenate([later[:n], later_turned], 0)
    ctrl_pair = jnp.concatenate([ctrl_slab, ctrl_turned], 0)
    ctrl_pairs = [ctrl_pair] + along(ctrl_pair)
    root = call(
        value_root_kernel,
        [((n, n), bf16)] * 2,
        [((n, n), bf16), ((n, n), f32)] + [((B, n), bf16)] * 2,
        24, 3 * 10**10, 1, order, *value_pairs,
    )
    root, trans_pair = lax.optimization_barrier((root, trans_pair))
    trans_pairs = [trans_pair] + along(trans_pair)
    wide = n + B
    gram, solved, back_side = call(
        inner_kernel,
        [((n, n), bf16), ((B, n), bf16), ((B, n), bf16)],
        [((n, n), f32)] + [((n, wide), bf16)] * 2
        + [((n, n + wide), f32)] + [((n, n + wide), bf16)] * 2 + [((B, n), bf16)] * 2
        + [((B, n), bf16)] * 2 + [((n // B, B, B), bf16)] * 2 + [((B, n), bf16)] * 2
        + [((B, n), f32)],
        42, 4 * 10**10, 1, order, *root, trans, *ctrl_pairs,
    )
    new_trans, new_ctrl, new_value = call(
        join_kernel, [((n, B), f32)] * 3, [((n, n), bf16)], 20, 10**10, 2,
        order, keep, gram, solved, back_side, trans, ctrl, value, later[n:], whole_t, *trans_pairs,
    )
    return new_trans[None], new_ctrl[None], new_value[None]


def solution(mesh):
    placed = (P("tm", None, "state"), P("tm", None, "state"), P("tm", None, "state"))
    return jax.shard_map(
        per_device, mesh=mesh, in_specs=placed, out_specs=placed, check_vma=False
    )
```

```python
import functools

import jax
import jax.numpy as jnp
from jax import lax
from jax.experimental import pallas as pl
from jax.experimental.pallas import tpu as pltpu
from jax.sharding import PartitionSpec as P

f32, bf16 = jnp.float32, jnp.bfloat16
B = 128
STEP = 32
CHUNK = 256
VMEM = pl.BlockSpec(memory_space=pltpu.VMEM)
SMEM = pl.BlockSpec(memory_space=pltpu.SMEM)


def halves(x):
    high = x.astype(bf16)
    return high, (x - high.astype(f32)).astype(bf16)


def product(a, b, ca=1, cb=0):
    return lax.dot_general(a, b, (((ca,), (cb,)), ((), ())), preferred_element_type=f32)


def product3(a, b, ca=1, cb=0):
    return product(a[0], b[0], ca, cb) + (product(a[0], b[1], ca, cb) + product(a[1], b[0], ca, cb))


def factor_block(block, work=()):
    sub = lax.broadcasted_iota(jnp.int32, (B, B), 0)
    ident = jnp.where(sub == lax.broadcasted_iota(jnp.int32, (B, B), 1), 1.0, 0.0).astype(f32)
    left = jnp.concatenate([block, ident], 1)
    lane = lax.broadcasted_iota(jnp.int32, (STEP, 2 * B), 1)
    row = lax.broadcasted_iota(jnp.int32, (STEP, 2 * B), 0)
    done, given = [], 0
    for first in range(0, B, STEP):
        piece = left[:STEP]
        cols = [
            jnp.broadcast_to(piece[:, first + k : first + k + 1], (STEP, B)) for k in range(STEP)
        ]
        rows = []
        for k in range(STEP):
            scale = lax.rsqrt(cols[k][k : k + 1])
            column = cols[k] * scale
            pivot_row = piece[k : k + 1] * jnp.concatenate([scale, scale], 1)
            rows.append(pivot_row)
            if k + 1 < STEP:
                for j in range(k + 1, STEP):
                    cols[j] = cols[j] - column * column[j : j + 1]
                piece = piece - jnp.concatenate([column, column], 1) * pivot_row
            while given < len(work) * (first + k + 1) // B:
                work[given]()
                given += 1
        upper = jnp.where(lane >= first + row, jnp.concatenate(rows, 0), 0.0)
        done.append(upper)
        if first + STEP < B:
            high, low = halves(upper)
            right = jnp.concatenate([high, low, high], 0)
            turned = jnp.concatenate([high[:, :B], high[:, :B], low[:, :B]], 0)
            left = left[STEP:] - product(turned, right, 0, 0)[first + STEP :]
    full = jnp.concatenate(done, 0)
    return full[:, :B], full[:, B:]


def chunks(first, last):
    return [(a, min(a + CHUNK, last)) for a in range(first, last, CHUNK)]


def eliminate(rows, high, low, turned, order, base, lead, finished=None, inverses=None):
    count, width = order // B, rows.shape[1]
    first_row = base(0)
    for piece in first_row[:lead]:
        piece()
    diagonal, work = rows[:B, :B], first_row[lead:] + base(1)
    for i in range(count):
        at, end = i * B, (i + 1) * B
        upper, inverse = factor_block(diagonal, work)
        work = []
        inverse = halves(inverse)
        if inverses is not None:
            inverses[0][i], inverses[1][i] = inverse
        high[at:end, at:end], low[at:end, at:end] = halves(upper)
        past, near_turned = end, None
        if i + 1 < count:
            past = end + B
            near = halves(product3(inverse, halves(rows[at:end, end:past])))
            high[at:end, end:past], low[at:end, end:past] = near
            near_turned = (near[0].T, near[1].T)
            diagonal = rows[end:past, end:past] - product3(near_turned, near)

        def far(a, b, at=at, end=end, inverse=inverse, near_turned=near_turned):
            part = halves(product3(inverse, halves(rows[at:end, a:b])))
            high[at:end, a:b], low[at:end, a:b] = part
            if near_turned is not None:
                rows[end : end + B, a:b] = rows[end : end + B, a:b] - product3(near_turned, part)

        work += [functools.partial(far, a, b) for a, b in chunks(past, width)]
        if i + 2 < count:
            work += base(i + 2)
            c = slice(end + B, end + 2 * B)

            def turn(end=end, c=c):
                turned[0][:, :end], turned[1][:, :end] = high[:end, c].T, low[:end, c].T

            def before(a, b, end=end, c=c):
                left = (turned[0][:, :end], turned[1][:, :end])
                rows[c, a:b] = rows[c, a:b] - product3(left, (high[:end, a:b], low[:end, a:b]))

            work.append(turn)
            work += [functools.partial(before, a, b) for a, b in chunks(end + B, width)]
        if finished is not None:
            work += finished(i)
    return work


def block_at(k):
    return pl.ds(pl.multiple_of(k * B, B), B)


def place(order, slabs, store):
    count = order.shape[0]
    share = count // 2 + 1
    for slot in range(count):
        k = order[slot]
        slab = slabs[slot // 2]
        for t in range(share):
            first = (slot % 2 * share + t) * B
            block = slab[first : first + B, :]
            j = lax.rem(k + t, count)
            store(j, k, block)
            if 0 < t < count // 2:
                store(k, j, block.T)


def value_root_kernel(order, *refs):
    slabs, (high, low, value, rows, turned_high, turned_low) = refs[:-6], refs[-6:]
    n = value.shape[0]

    def store(j, k, block):
        value[block_at(j), block_at(k)] = block

    place(order, slabs, store)

    def base(i):
        def widen():
            rows[i * B : (i + 1) * B, i * B :] = value[i * B : (i + 1) * B, i * B :].astype(f32)

        return [widen]

    eliminate(rows, high, low, (turned_high, turned_low), n, base, 1)


def inner_kernel(order, root_high, root_low, trans, *refs):
    slabs, refs = refs[:4], refs[4:]
    gram_out, solved_out, back_out = refs[:3]
    gram, side_high, side_low, rows, high, low, turned_high, turned_low = refs[3:11]
    left_high, left_low, inverse_high, inverse_low, back_high, back_low, back = refs[11:]
    n = root_high.shape[0]
    count = n // B

    def store(j, k, block):
        gram[block_at(j), block_at(k)] = block
        side_high[block_at(j), block_at(k)], side_low[block_at(j), block_at(k)] = halves(block)

    place(order, slabs, store)
    side_high[:, n:], side_low[:, n:] = halves(trans[...])
    sub = lax.broadcasted_iota(jnp.int32, (B, B), 0)
    ident = jnp.where(sub == lax.broadcasted_iota(jnp.int32, (B, B), 1), 1.0, 0.0).astype(f32)

    def base(i):
        at, end = i * B, (i + 1) * B

        def couple(a, b):
            part = product3(
                (root_high[at:end, at:], root_low[at:end, at:]),
                (side_high[at:, a:b], side_low[at:, a:b]),
            )
            rows[at:end, n + a : n + b] = part
            if a < n:
                left_high[:, a:b], left_low[:, a:b] = halves(part)

        def inner(j):
            c = slice(j * B, (j + 1) * B)
            part = product3(
                (left_high[:, j * B :], left_low[:, j * B :]),
                (root_high[c, j * B :], root_low[c, j * B :]),
                1,
                1,
            )
            rows[at:end, c] = part + ident if j == i else part

        work = [functools.partial(couple, a, b) for a, b in chunks(0, n)]
        work += [functools.partial(inner, j) for j in range(i, count)]
        return work + [functools.partial(couple, n, n + B)]

    def subtract(first, last, r, out):
        c = slice(r, r + B)
        out[c, :] = (
            gram[c, :] - product(high[first:last, n + r : n + r + B], high[first:last, n : 2 * n], 0, 0)
        ).astype(out.dtype)

    def finished(i):
        first, last = (i - 1) * B, (i + 1) * B
        if i == count - 2:
            first = i * B
        elif i % 2 == 0 or i == count - 1:
            return []
        return [functools.partial(subtract, first, last, r, gram) for r in range(0, n, B)]

    work = eliminate(
        rows, high, low, (turned_high, turned_low), n, base, len(chunks(0, n)) + 1, finished,
        (inverse_high, inverse_low),
    )

    def solve(a, b):
        solved_out[:, a:b] = (
            trans[a:b, :].T - product(high[:, 2 * n :], high[:, n + a : n + b], 0, 0)
        ).astype(bf16)

    def behind(i, j):
        part = (back_high[:, j * B :], back_low[:, j * B :])
        c = slice(i * B, (i + 1) * B)
        return product3(part, (high[c, j * B : n], low[c, j * B : n]), 1, 1)

    work.pop()()
    work += [functools.partial(subtract, n - B, n, r, gram_out) for r in range(0, n, B)]
    work += [functools.partial(solve, a, b) for a, b in chunks(0, n)]
    share = -(-len(work) // count)
    part = high[n - B : n, 2 * n :].T.astype(f32)
    for i in reversed(range(count)):
        at, end = i * B, (i + 1) * B
        later_part = None
        if i > 0:
            later_part = high[at - B : at, 2 * n :].T.astype(f32)
            if end < n:
                later_part = later_part - behind(i - 1, i + 1)
        found = halves(product3(halves(part), (inverse_high[i], inverse_low[i])))
        back_high[:, at:end], back_low[:, at:end] = found
        if i > 0:
            c = slice(at - B, at)
            part = later_part - product3(found, (high[c, at:end], low[c, at:end]), 1, 1)
        added = product3(found, (root_high[at:end, at:], root_low[at:end, at:]))
        if end < n:
            back[:, at:end] = added[:, :B]
            back[:, end:] = back[:, end:] + added[:, B:]
        else:
            back[:, at:] = added
        for piece in work[:share]:
            piece()
        work = work[share:]
    back_out[...] = back[...].astype(bf16)


def join_kernel(order, keep, gram, solved, trans, ctrl, later_c, *refs):
    pairs, (trans_out, ctrl_out, later_t) = refs[:-3], refs[-3:]
    n = trans.shape[0]
    kept = keep[0] > 0
    for slot in range(order.shape[0]):
        block = pairs[slot // 2][slot % 2 * n : (slot % 2 + 1) * n, :]
        later_t[:, block_at(order[slot])] = block
    mapped = product(later_t[block_at(order[0]), :], gram[...]).astype(bf16)
    joined = product(later_t[...], jnp.concatenate([solved[...], mapped], 0), 1, 1)
    trans_out[...] = jnp.where(kept, trans[...], joined[:, :B])
    ctrl_out[...] = jnp.where(kept, ctrl[...], later_c[...].astype(f32) + joined[:, B:])


def value_kernel(keep, back, whole_t, value, value_out):
    added = product(back[...], whole_t[...]).T
    value_out[...] = jnp.where(keep[0] > 0, 0.0, added) + value[...]


def slab_kernel(order, whole, out):
    count = order.shape[0]
    for t in range(count // 2 + 1):
        out[t * B : (t + 1) * B, :] = whole[block_at(lax.rem(order[0] + t, count)), :].astype(out.dtype)


def call(kernel, outs, scratch, megabytes, flops, smem, *args):
    return pl.pallas_call(
        kernel,
        out_shape=[jax.ShapeDtypeStruct(shape, kind) for shape, kind in outs],
        in_specs=[SMEM] * smem + [VMEM] * (len(args) - smem),
        out_specs=[VMEM] * len(outs),
        scratch_shapes=[pltpu.VMEM(shape, kind) for shape, kind in scratch],
        compiler_params=pltpu.CompilerParams(vmem_limit_bytes=megabytes << 20),
        cost_estimate=pl.CostEstimate(flops=flops, bytes_accessed=1 << 20, transcendentals=0),
    )(*args)


def turn(s):
    return s // 2 * 2 + (s + 1) % 2


def along(pair):
    return [
        lax.ppermute(pair, "state", [(s, (s // 2 + hop) % 4 * 2 + s % 2) for s in range(8)])
        for hop in (1, 3, 2)
    ]


def sources():
    state = lax.axis_index("state")
    y, x = state // 2, state % 2
    found = []
    for hop in (0, 1, 3, 2):
        found += [(y - hop + 4) % 4 * 2 + x, (y - hop + 4) % 4 * 2 + 1 - x]
    return jnp.stack(found).astype(jnp.int32)


def per_device(transition, control_gram, value_gram):
    trans, ctrl, value = transition[0], control_gram[0], value_gram[0]
    n = trans.shape[0]
    count = lax.axis_size("tm")
    back = [((t + 1) % count, t) for t in range(count)]
    back_turned = [
        ((t + 1) % count * 8 + turn(s), t * 8 + s) for t in range(count) for s in range(8)
    ]
    keep = (lax.axis_index("tm") == count - 1).astype(jnp.int32)[None]
    order = sources()
    turned = [(s, turn(s)) for s in range(8)]

    def slab(whole, kind):
        (share,) = call(slab_kernel, [((n // 2 + B, B), kind)], [], 62, 10**8, 1, order, whole)
        return share

    value_slab = slab(value, bf16)
    later_v = [
        lax.ppermute(value_slab, "tm", back),
        lax.ppermute(value_slab, ("tm", "state"), back_turned),
    ]
    ctrl_slab = slab(ctrl, f32)
    ctrl_turned = lax.ppermute(ctrl_slab, "state", turned)
    later_v, late_trans, late_ctrl = lax.optimization_barrier((later_v, trans, ctrl))
    trans_b = late_trans.astype(bf16)
    whole_t = lax.all_gather(trans_b, "state", axis=1, tiled=True)
    value_pair = jnp.concatenate(later_v, 0)
    value_pairs = [value_pair] + along(value_pair)
    later = lax.ppermute(jnp.concatenate([trans_b, late_ctrl.astype(bf16)], 0), "tm", back)
    later_turned = lax.ppermute(trans_b, ("tm", "state"), back_turned)
    trans_pair = jnp.concatenate([later[:n], later_turned], 0)
    ctrl_pair = jnp.concatenate([ctrl_slab, ctrl_turned], 0)
    ctrl_pairs = [ctrl_pair] + along(ctrl_pair)
    root = call(
        value_root_kernel,
        [((n, n), bf16)] * 2,
        [((n, n), bf16), ((n, n), f32)] + [((B, n), bf16)] * 2,
        24, 3 * 10**10, 1, order, *value_pairs,
    )
    root, trans_pair = lax.optimization_barrier((root, trans_pair))
    trans_pairs = [trans_pair] + along(trans_pair)
    wide = n + B
    gram, solved, back_side = call(
        inner_kernel,
        [((n, n), bf16), ((B, n), bf16), ((B, n), bf16)],
        [((n, n), f32)] + [((n, wide), bf16)] * 2
        + [((n, n + wide), f32)] + [((n, n + wide), bf16)] * 2 + [((B, n), bf16)] * 2
        + [((B, n), bf16)] * 2 + [((n // B, B, B), bf16)] * 2 + [((B, n), bf16)] * 2
        + [((B, n), f32)],
        42, 4 * 10**10, 1, order, *root, trans, *ctrl_pairs,
    )
    new_trans, new_ctrl = call(
        join_kernel, [((n, B), f32)] * 2, [((n, n), bf16)], 20, 10**10, 2,
        order, keep, gram, solved, trans, ctrl, later[n:], *trans_pairs,
    )
    (new_value,) = call(
        value_kernel, [((n, B), f32)], [], 62, 10**9, 1, keep, back_side, whole_t, value
    )
    return new_trans[None], new_ctrl[None], new_value[None]


def solution(mesh):
    placed = (P("tm", None, "state"), P("tm", None, "state"), P("tm", None, "state"))
    return jax.shard_map(
        per_device, mesh=mesh, in_specs=placed, out_specs=placed, check_vma=False
    )
```

```python
import functools

import jax
import jax.numpy as jnp
from jax import lax
from jax.experimental import pallas as pl
from jax.experimental.pallas import tpu as pltpu
from jax.sharding import PartitionSpec as P

f32, bf16 = jnp.float32, jnp.bfloat16
B = 128
STEP = 32
CHUNK = 256
VMEM = pl.BlockSpec(memory_space=pltpu.VMEM)
SMEM = pl.BlockSpec(memory_space=pltpu.SMEM)


def halves(x):
    high = x.astype(bf16)
    return high, (x - high.astype(f32)).astype(bf16)


def product(a, b, ca=1, cb=0):
    return lax.dot_general(a, b, (((ca,), (cb,)), ((), ())), preferred_element_type=f32)


def product3(a, b, ca=1, cb=0):
    return product(a[0], b[0], ca, cb) + (product(a[0], b[1], ca, cb) + product(a[1], b[0], ca, cb))


def factor_block(block, work=()):
    sub = lax.broadcasted_iota(jnp.int32, (B, B), 0)
    ident = jnp.where(sub == lax.broadcasted_iota(jnp.int32, (B, B), 1), 1.0, 0.0).astype(f32)
    left = jnp.concatenate([block, ident], 1)
    lane = lax.broadcasted_iota(jnp.int32, (STEP, 2 * B), 1)
    row = lax.broadcasted_iota(jnp.int32, (STEP, 2 * B), 0)
    done, given = [], 0
    for first in range(0, B, STEP):
        piece = left[:STEP]
        cols = [
            jnp.broadcast_to(piece[:, first + k : first + k + 1], (STEP, B)) for k in range(STEP)
        ]
        rows = []
        for k in range(STEP):
            scale = lax.rsqrt(cols[k][k : k + 1])
            column = cols[k] * scale
            pivot_row = piece[k : k + 1] * jnp.concatenate([scale, scale], 1)
            rows.append(pivot_row)
            if k + 1 < STEP:
                for j in range(k + 1, STEP):
                    cols[j] = cols[j] - column * column[j : j + 1]
                piece = piece - jnp.concatenate([column, column], 1) * pivot_row
            while given < len(work) * (first + k + 1) // B:
                work[given]()
                given += 1
        upper = jnp.where(lane >= first + row, jnp.concatenate(rows, 0), 0.0)
        done.append(upper)
        if first + STEP < B:
            high, low = halves(upper)
            right = jnp.concatenate([high, low, high], 0)
            turned = jnp.concatenate([high[:, :B], high[:, :B], low[:, :B]], 0)
            left = left[STEP:] - product(turned, right, 0, 0)[first + STEP :]
    full = jnp.concatenate(done, 0)
    return full[:, :B], full[:, B:]


def chunks(first, last):
    return [(a, min(a + CHUNK, last)) for a in range(first, last, CHUNK)]


def eliminate(rows, high, low, turned, order, base, lead, finished=None, inverses=None):
    count, width = order // B, rows.shape[1]
    first_row = base(0)
    for piece in first_row[:lead]:
        piece()
    diagonal, work = rows[:B, :B], first_row[lead:] + base(1)
    for i in range(count):
        at, end = i * B, (i + 1) * B
        upper, inverse = factor_block(diagonal, work)
        work = []
        inverse = halves(inverse)
        if inverses is not None:
            inverses[0][i], inverses[1][i] = inverse
        high[at:end, at:end], low[at:end, at:end] = halves(upper)
        past, near_turned = end, None
        if i + 1 < count:
            past = end + B
            near = halves(product3(inverse, halves(rows[at:end, end:past])))
            high[at:end, end:past], low[at:end, end:past] = near
            near_turned = (near[0].T, near[1].T)
            diagonal = rows[end:past, end:past] - product3(near_turned, near)

        def far(a, b, at=at, end=end, inverse=inverse, near_turned=near_turned):
            part = halves(product3(inverse, halves(rows[at:end, a:b])))
            high[at:end, a:b], low[at:end, a:b] = part
            if near_turned is not None:
                rows[end : end + B, a:b] = rows[end : end + B, a:b] - product3(near_turned, part)

        work += [functools.partial(far, a, b) for a, b in chunks(past, width)]
        if i + 2 < count:
            work += base(i + 2)
            c = slice(end + B, end + 2 * B)

            def turn(end=end, c=c):
                turned[0][:, :end], turned[1][:, :end] = high[:end, c].T, low[:end, c].T

            def before(a, b, end=end, c=c):
                left = (turned[0][:, :end], turned[1][:, :end])
                rows[c, a:b] = rows[c, a:b] - product3(left, (high[:end, a:b], low[:end, a:b]))

            work.append(turn)
            work += [functools.partial(before, a, b) for a, b in chunks(end + B, width)]
        if finished is not None:
            work += finished(i)
    return work


def block_at(k):
    return pl.ds(pl.multiple_of(k * B, B), B)


def place(order, slabs, store):
    count = order.shape[0]
    share = count // 2 + 1
    for slot in range(count):
        k = order[slot]
        slab = slabs[slot // 2]
        for t in range(share):
            first = (slot % 2 * share + t) * B
            block = slab[first : first + B, :]
            j = lax.rem(k + t, count)
            store(j, k, block)
            if 0 < t < count // 2:
                store(k, j, block.T)


def value_root_kernel(order, *refs):
    slabs, (high, low, value, rows, turned_high, turned_low) = refs[:-6], refs[-6:]
    n = value.shape[0]

    def store(j, k, block):
        value[block_at(j), block_at(k)] = block

    place(order, slabs, store)

    def base(i):
        def widen():
            rows[i * B : (i + 1) * B, i * B :] = value[i * B : (i + 1) * B, i * B :].astype(f32)

        return [widen]

    eliminate(rows, high, low, (turned_high, turned_low), n, base, 1)


def inner_kernel(order, root_high, root_low, trans, *refs):
    slabs, refs = refs[:4], refs[4:]
    gram_out, solved_out, back_out = refs[:3]
    gram, side_high, side_low, rows, high, low, turned_high, turned_low = refs[3:11]
    left_high, left_low, inverse_high, inverse_low, back_high, back_low, back = refs[11:]
    n = root_high.shape[0]
    count = n // B

    def store(j, k, block):
        gram[block_at(j), block_at(k)] = block
        side_high[block_at(j), block_at(k)], side_low[block_at(j), block_at(k)] = halves(block)

    place(order, slabs, store)
    side_high[:, n:], side_low[:, n:] = halves(trans[...])
    sub = lax.broadcasted_iota(jnp.int32, (B, B), 0)
    ident = jnp.where(sub == lax.broadcasted_iota(jnp.int32, (B, B), 1), 1.0, 0.0).astype(f32)

    def base(i):
        at, end = i * B, (i + 1) * B

        def couple(a, b):
            part = product3(
                (root_high[at:end, at:], root_low[at:end, at:]),
                (side_high[at:, a:b], side_low[at:, a:b]),
            )
            rows[at:end, n + a : n + b] = part
            if a < n:
                left_high[:, a:b], left_low[:, a:b] = halves(part)

        def inner(j):
            c = slice(j * B, (j + 1) * B)
            part = product3(
                (left_high[:, j * B :], left_low[:, j * B :]),
                (root_high[c, j * B :], root_low[c, j * B :]),
                1,
                1,
            )
            rows[at:end, c] = part + ident if j == i else part

        work = [functools.partial(couple, a, b) for a, b in chunks(0, n)]
        work += [functools.partial(inner, j) for j in range(i, count)]
        return work + [functools.partial(couple, n, n + B)]

    def subtract(first, last, r, out):
        c = slice(r, r + B)
        out[c, :] = (
            gram[c, :] - product(high[first:last, n + r : n + r + B], high[first:last, n : 2 * n], 0, 0)
        ).astype(out.dtype)

    def finished(i):
        first, last = (i - 1) * B, (i + 1) * B
        if i == count - 2:
            first = i * B
        elif i % 2 == 0 or i == count - 1:
            return []
        return [functools.partial(subtract, first, last, r, gram) for r in range(0, n, B)]

    work = eliminate(
        rows, high, low, (turned_high, turned_low), n, base, len(chunks(0, n)) + 1, finished,
        (inverse_high, inverse_low),
    )

    def solve(a, b):
        solved_out[:, a:b] = (
            trans[a:b, :].T - product(high[:, 2 * n :], high[:, n + a : n + b], 0, 0)
        ).astype(bf16)

    def behind(i, j):
        part = (back_high[:, j * B :], back_low[:, j * B :])
        c = slice(i * B, (i + 1) * B)
        return product3(part, (high[c, j * B : n], low[c, j * B : n]), 1, 1)

    work.pop()()
    work += [functools.partial(subtract, n - B, n, r, gram_out) for r in range(0, n, B)]
    work += [functools.partial(solve, a, b) for a, b in chunks(0, n)]
    share = -(-len(work) // count)
    part = high[n - B : n, 2 * n :].T.astype(f32)
    for i in reversed(range(count)):
        at, end = i * B, (i + 1) * B
        later_part = None
        if i > 0:
            later_part = high[at - B : at, 2 * n :].T.astype(f32)
            if end < n:
                later_part = later_part - behind(i - 1, i + 1)
        found = halves(product3(halves(part), (inverse_high[i], inverse_low[i])))
        back_high[:, at:end], back_low[:, at:end] = found
        if i > 0:
            c = slice(at - B, at)
            part = later_part - product3(found, (high[c, at:end], low[c, at:end]), 1, 1)
        added = product3(found, (root_high[at:end, at:], root_low[at:end, at:]))
        if end < n:
            back[:, at:end] = added[:, :B]
            back[:, end:] = back[:, end:] + added[:, B:]
        else:
            back[:, at:] = added
        for piece in work[:share]:
            piece()
        work = work[share:]
    back_out[...] = back[...].astype(bf16)


def join_kernel(order, keep, gram, solved, trans, ctrl, later_c, *refs):
    pairs, (trans_out, ctrl_out, later_t) = refs[:-3], refs[-3:]
    n = trans.shape[0]
    kept = keep[0] > 0
    for slot in range(order.shape[0]):
        block = pairs[slot // 2][slot % 2 * n : (slot % 2 + 1) * n, :]
        later_t[:, block_at(order[slot])] = block
    mapped = product(later_t[block_at(order[0]), :], gram[...]).astype(bf16)
    joined = product(later_t[...], jnp.concatenate([solved[...], mapped], 0), 1, 1)
    trans_out[...] = jnp.where(kept, trans[...], joined[:, :B])
    ctrl_out[...] = jnp.where(kept, ctrl[...], later_c[...].astype(f32) + joined[:, B:])


def value_kernel(keep, back, whole_t, value, value_out):
    added = product(back[...], whole_t[...]).T
    value_out[...] = jnp.where(keep[0] > 0, 0.0, added) + value[...]


def slab_kernel(order, whole, out):
    count = order.shape[0]
    for t in range(count // 2 + 1):
        out[t * B : (t + 1) * B, :] = whole[block_at(lax.rem(order[0] + t, count)), :].astype(out.dtype)


def call(kernel, outs, scratch, megabytes, flops, smem, *args):
    return pl.pallas_call(
        kernel,
        out_shape=[jax.ShapeDtypeStruct(shape, kind) for shape, kind in outs],
        in_specs=[SMEM] * smem + [VMEM] * (len(args) - smem),
        out_specs=[VMEM] * len(outs),
        scratch_shapes=[pltpu.VMEM(shape, kind) for shape, kind in scratch],
        compiler_params=pltpu.CompilerParams(vmem_limit_bytes=megabytes << 20),
        cost_estimate=pl.CostEstimate(flops=flops, bytes_accessed=1 << 20, transcendentals=0),
    )(*args)


def turn(s):
    return s // 2 * 2 + (s + 1) % 2


def along(pair):
    return [
        lax.ppermute(pair, "state", [(s, (s // 2 + hop) % 4 * 2 + s % 2) for s in range(8)])
        for hop in (2, 1, 3)
    ]


def sources():
    state = lax.axis_index("state")
    y, x = state // 2, state % 2
    found = []
    for hop in (0, 2, 1, 3):
        found += [(y - hop + 4) % 4 * 2 + x, (y - hop + 4) % 4 * 2 + 1 - x]
    return jnp.stack(found).astype(jnp.int32)


def per_device(transition, control_gram, value_gram):
    trans, ctrl, value = transition[0], control_gram[0], value_gram[0]
    n = trans.shape[0]
    count = lax.axis_size("tm")
    back = [((t + 1) % count, t) for t in range(count)]
    back_turned = [
        ((t + 1) % count * 8 + turn(s), t * 8 + s) for t in range(count) for s in range(8)
    ]
    keep = (lax.axis_index("tm") == count - 1).astype(jnp.int32)[None]
    order = sources()
    turned = [(s, turn(s)) for s in range(8)]

    def slab(whole, kind):
        (share,) = call(slab_kernel, [((n // 2 + B, B), kind)], [], 16, 10**8, 1, order, whole)
        return share

    value_slab = slab(value, bf16)
    later_v = [
        lax.ppermute(value_slab, "tm", back),
        lax.ppermute(value_slab, ("tm", "state"), back_turned),
    ]
    ctrl_slab = slab(ctrl, f32)
    ctrl_turned = lax.ppermute(ctrl_slab, "state", turned)
    later_v, late_trans, late_ctrl = lax.optimization_barrier((later_v, trans, ctrl))
    trans_b = late_trans.astype(bf16)
    value_pair = jnp.concatenate(later_v, 0)
    value_pairs = [value_pair] + along(value_pair)
    value_pairs, here_t = lax.optimization_barrier((value_pairs, trans_b))
    whole_t = lax.all_gather(here_t, "state", axis=1, tiled=True)
    later = lax.ppermute(jnp.concatenate([trans_b, late_ctrl.astype(bf16)], 0), "tm", back)
    later_turned = lax.ppermute(trans_b, ("tm", "state"), back_turned)
    trans_pair = jnp.concatenate([later[:n], later_turned], 0)
    ctrl_pair = jnp.concatenate([ctrl_slab, ctrl_turned], 0)
    ctrl_pairs = [ctrl_pair] + along(ctrl_pair)
    root = call(
        value_root_kernel,
        [((n, n), bf16)] * 2,
        [((n, n), bf16), ((n, n), f32)] + [((B, n), bf16)] * 2,
        24, 3 * 10**10, 1, order, *value_pairs,
    )
    root, trans_pair = lax.optimization_barrier((root, trans_pair))
    trans_pairs = [trans_pair] + along(trans_pair)
    wide = n + B
    gram, solved, back_side = call(
        inner_kernel,
        [((n, n), bf16), ((B, n), bf16), ((B, n), bf16)],
        [((n, n), f32)] + [((n, wide), bf16)] * 2
        + [((n, n + wide), f32)] + [((n, n + wide), bf16)] * 2 + [((B, n), bf16)] * 2
        + [((B, n), bf16)] * 2 + [((n // B, B, B), bf16)] * 2 + [((B, n), bf16)] * 2
        + [((B, n), f32)],
        42, 4 * 10**10, 1, order, *root, trans, *ctrl_pairs,
    )
    new_trans, new_ctrl = call(
        join_kernel, [((n, B), f32)] * 2, [((n, n), bf16)], 20, 10**10, 2,
        order, keep, gram, solved, trans, ctrl, later[n:], *trans_pairs,
    )
    (new_value,) = call(
        value_kernel, [((n, B), f32)], [], 62, 10**9, 1, keep, back_side, whole_t, value
    )
    return new_trans[None], new_ctrl[None], new_value[None]


def solution(mesh):
    placed = (P("tm", None, "state"), P("tm", None, "state"), P("tm", None, "state"))
    return jax.shard_map(
        per_device, mesh=mesh, in_specs=placed, out_specs=placed, check_vma=False
    )
```
